32 devices in a mesh: rep: 8 (over z, core), seq: 4 (over y, x).
Axes of the slice: x: 2, y: 2, z: 4, core: 2. Of those that a mesh axis runs over, the one named last changes fastest.
Arguments:
- latent: bfloat16 [768, 2432], P(('seq', 'rep')), may hold values from -50 to 50
- noise: bfloat16 [8, 768, 2432], P('rep', 'seq'), may hold values from -6 to 6
- timestep: int32 [8], P('rep'), may hold values from 10 to 989
- text_kv: bfloat16 [2, 128, 1536], P(None, None, 'seq'), may hold values from -6 to 6
- qk_gain: float32 [2, 64], replicated, may hold values from 1 to 3
- prompt: float32 [1280], replicated, may hold values from -6 to 6
- w_qkv: bfloat16 [2432, 4608], P('rep'), may hold values from -0.125 to 0.125
- a_qkv: bfloat16 [2432, 64], replicated, may hold values from -0.125 to 0.125
- b_qkv: bfloat16 [64, 4608], replicated, may hold values from -0.75 to 0.75
- w_out: bfloat16 [1536, 2432], P('rep'), may hold values from -0.15625 to 0.15625
- a_out: bfloat16 [1536, 64], replicated, may hold values from -0.15625 to 0.15625
- b_out: bfloat16 [64, 2432], replicated, may hold values from -0.75 to 0.75
- w_patch: bfloat16 [2432, 1280], replicated, may hold values from -0.125 to 0.125
Outputs:
- rewards: float32 [8], P('rep')
- latent_grad: float32 [768, 2432], P(('seq', 'rep'))
- grad_a_qkv: float32 [2432, 64], P('rep')
- grad_b_qkv: float32 [64, 4608], P(None, 'rep')
- grad_a_out: float32 [1536, 64], P('rep')
- grad_b_out: float32 [64, 2432], P(None, 'rep')
The draws below stay inside these ranges and needn't reach their ends.
All inputs are finite; a program needn't handle non-finite values.
Results may differ from the reference program's by a relative error of at most 0.024.
Values may be sent and summed in bfloat16 or wider, within the bound.
A program may use at most 192 MiB of HBM per device.

```python
import math
import jax
import jax.numpy as jnp
from jax import lax

D = 2432
HEAD_DIM = 64
RANK = 64
VW = 1280
TXT = 128
HD = 1536
TOKENS = 768
REPS = 8


def draw_latent(key, part):
    first, second = jax.random.split(key, 2)
    positions = jnp.arange(TOKENS, dtype=jnp.float32)
    rising = jnp.exp(jnp.log(3.0) * positions / TOKENS)
    jitter = jnp.exp(jax.random.uniform(first, (TOKENS,), minval=0.0, maxval=jnp.log(10.0 / 3.0)))
    row_scale = (rising * jitter)[:, None]
    values = jnp.clip(jax.random.normal(second, (TOKENS, D)), -4.0, 4.0)
    return (values * row_scale).astype(jnp.float32).astype(jnp.bfloat16)


def touch_ends(result, own_key, smallest, high):
    index_at = [jax.random.randint(jax.random.fold_in(own_key, axis), (), 0, length) for axis, length in enumerate(result.shape)]
    widest = result.shape.index(max(result.shape))
    beside = index_at[:widest] + [(index_at[widest] + 1) % result.shape[widest]] + index_at[widest + 1:]
    return result.at[tuple(index_at)].set(smallest).at[tuple(beside)].set(high)


def spiked(array, stream_key, source, target, blocks, factor):
    def block_of(position):
        return (jnp.arange(array.shape[position]) // (array.shape[position] // blocks)).reshape((-1,) + (1,) * (array.ndim - 1 - position))

    one_side = jax.random.permutation(stream_key, blocks)[block_of(target)]
    far = (block_of(target) + blocks // 2) % blocks
    return jnp.where((block_of(source) == one_side) | (block_of(source) == far), factor * array, array)


def level_of(key, shape, shards, smallest, top_value):
    def one(dim, blocks):
        steps = jax.random.uniform(jax.random.fold_in(jax.random.fold_in(key, 6), dim), (blocks,), jnp.float32, smallest / len(shards), top_value / len(shards))
        return jnp.repeat(jnp.exp(steps), shape[dim] // blocks).reshape((-1,) + (1,) * (len(shape) - dim - 1))

    level = one(*shards[0])
    for cut in shards[1:]:
        level = level * one(*cut)
    return level


def normal_values(stream_key, shape, spread, bound, pieces=(), kind=jnp.bfloat16):
    loudness = level_of(stream_key, shape, pieces, -0.22, 0.18) if pieces else 1.0
    entries = jax.random.normal(stream_key, shape, jnp.float32) * spread * loudness
    return jnp.minimum(jnp.maximum(entries, -bound), bound).astype(kind)


def heavy_noise(own_key, extent, width, reach, cuts, heavy, held_as=jnp.bfloat16):
    values = width * jax.random.normal(own_key, extent, jnp.float32)
    if cuts:
        values = values * level_of(own_key, extent, cuts, -0.22, 0.18)
    return jnp.clip(spiked(values, jax.random.fold_in(own_key, 3), *heavy), -reach, reach).astype(held_as)


def setup_inputs(seed: int = 0) -> dict:
    splits = jax.random.split(jax.random.key(seed), 14)
    latent = draw_latent(jax.random.fold_in(splits[13], 71), 0)
    noise = heavy_noise(splits[1], (REPS, TOKENS, D), 1.0, 6.0, ((0, 8), (1, 4)), (0, 1, 8, 2.0))
    timestep = touch_ends(jax.random.randint(splits[2], (REPS,), 10, 990), jax.random.fold_in(splits[2], 1), 10, 989).astype(jnp.int32)
    text_kv = normal_values(splits[3], (2, TXT, HD), 1.0, 6.0, ((2, 4),))
    qk_gain = jnp.clip(jnp.exp(jax.random.uniform(splits[4], (2, HEAD_DIM), jnp.float32, math.log(1.0), math.log(3.0))), 1.0, 3.0)
    prompt = normal_values(splits[5], (VW,), 1.0, 6.0, (), jnp.float32)
    w_qkv = normal_values(splits[6], (D, 3 * HD), D ** -0.5, 0.125, ((0, 8),))
    a_qkv = normal_values(splits[7], (D, RANK), D ** -0.5, 0.125)
    b_qkv = normal_values(splits[8], (RANK, 3 * HD), RANK ** -0.5, 0.75)
    w_out = normal_values(splits[9], (HD, D), HD ** -0.5, 0.15625, ((0, 8),))
    a_out = normal_values(splits[10], (HD, RANK), HD ** -0.5, 0.15625)
    b_out = normal_values(splits[11], (RANK, D), RANK ** -0.5, 0.75)
    w_patch = normal_values(splits[12], (D, VW), D ** -0.5, 0.125)
    return {"latent": latent, "noise": noise, "timestep": timestep, "text_kv": text_kv, "qk_gain": qk_gain, "prompt": prompt, "w_qkv": w_qkv, "a_qkv": a_qkv, "b_qkv": b_qkv, "w_out": w_out, "a_out": a_out, "b_out": b_out, "w_patch": w_patch}


epsilon = 1e-06
logit_scale = 100.0
contract_last = (((1,), (1,)), ((), ()))
contract_first = (((0,), (0,)), ((), ()))

def layer_norm(mixed_in):
    centred = mixed_in - lax.optimization_barrier(jnp.mean(mixed_in, axis=-1, keepdims=True))
    return centred * lax.rsqrt(lax.optimization_barrier(jnp.mean(centred * centred, axis=-1, keepdims=True)) + epsilon)

def head_norm(values_in, norm_gain, head_size):
    leading = values_in.shape[0]
    shaped = values_in.reshape(leading, -1, head_size)
    scaled = shaped * lax.rsqrt(lax.optimization_barrier(jnp.mean(shaped * shaped, axis=-1, keepdims=True)) + epsilon)
    return (scaled * norm_gain).reshape(leading, -1)

def split_heads(matrix, head_size):
    return jnp.transpose(matrix.reshape(matrix.shape[0], -1, head_size), (1, 0, 2))

def merge_heads(blocks):
    return jnp.transpose(blocks, (1, 0, 2)).reshape(blocks.shape[1], -1)

def project_in(latent_rows, noise_rows, noise_level, w_qkv, a_qkv, b_qkv, qk_gain, head_size):
    mixed_in = (1.0 - noise_level) * latent_rows.astype(jnp.float32) + noise_level * noise_rows.astype(jnp.float32)
    normed = layer_norm(mixed_in).astype(jnp.bfloat16)
    low_rank = jnp.dot(normed, a_qkv, preferred_element_type=jnp.float32).astype(jnp.bfloat16)
    joined_qkv = jnp.dot(normed, w_qkv, preferred_element_type=jnp.float32) + jnp.dot(low_rank, b_qkv, preferred_element_type=jnp.float32)
    inner_width = joined_qkv.shape[1] // 3
    query_part = head_norm(joined_qkv[:, :inner_width], qk_gain[0], head_size)
    key_part = head_norm(joined_qkv[:, inner_width:2 * inner_width], qk_gain[1], head_size)
    stacked = jnp.stack([query_part, key_part, joined_qkv[:, 2 * inner_width:]], axis=1).astype(jnp.bfloat16)
    return (mixed_in, normed, low_rank, joined_qkv, stacked)

def head_scores(query_head, key_head, head_size):
    logits = lax.dot_general(query_head, key_head, contract_last, preferred_element_type=jnp.float32) / math.sqrt(head_size)
    expped = jnp.exp(logits)
    return expped / lax.optimization_barrier(jnp.sum(expped, axis=1, keepdims=True))

def attend(stacked, text_keys, text_values, head_size):
    query_heads = split_heads(stacked[:, 0], head_size)
    key_heads = split_heads(jnp.concatenate([stacked[:, 1], text_keys], axis=0), head_size)
    value_heads = split_heads(jnp.concatenate([stacked[:, 2], text_values], axis=0), head_size)

    def one_head(inputs):
        query_head, key_head, value_head = inputs
        rounded = head_scores(query_head, key_head, head_size).astype(jnp.bfloat16)
        return jnp.dot(rounded, value_head, preferred_element_type=jnp.float32).astype(jnp.bfloat16)
    return merge_heads(lax.map(one_head, (query_heads, key_heads, value_heads)))

def attend_back(stacked, text_keys, text_values, grad_attended, head_size):
    tokens_all = stacked.shape[0]
    query_heads = split_heads(stacked[:, 0], head_size)
    key_heads = split_heads(jnp.concatenate([stacked[:, 1], text_keys], axis=0), head_size)
    value_heads = split_heads(jnp.concatenate([stacked[:, 2], text_values], axis=0), head_size)
    grad_heads = split_heads(grad_attended, head_size)

    def one_head(inputs):
        query_head, key_head, value_head, grad_head = inputs
        soft_probs = head_scores(query_head, key_head, head_size)
        rounded = soft_probs.astype(jnp.bfloat16)
        grad_values = lax.dot_general(rounded, grad_head, contract_first, preferred_element_type=jnp.float32)
        grad_probs = lax.dot_general(grad_head, value_head, contract_last, preferred_element_type=jnp.float32)
        centre = lax.optimization_barrier(jnp.sum(soft_probs * grad_probs, axis=1, keepdims=True))
        grad_logits = (soft_probs * (grad_probs - centre) / math.sqrt(head_size)).astype(jnp.bfloat16)
        grad_query = jnp.dot(grad_logits, key_head, preferred_element_type=jnp.float32)
        grad_keys = lax.dot_general(grad_logits, query_head, contract_first, preferred_element_type=jnp.float32)
        return jnp.stack([grad_query, grad_keys[:tokens_all], grad_values[:tokens_all]], axis=0)
    per_head = lax.map(one_head, (query_heads, key_heads, value_heads, grad_heads))
    return jnp.transpose(per_head, (2, 1, 0, 3)).reshape(tokens_all, 3, -1).astype(jnp.bfloat16)

def project_out(attended, mixed_in, noise_level, w_out, a_out, b_out, w_patch):
    low_out = jnp.dot(attended, a_out, preferred_element_type=jnp.float32).astype(jnp.bfloat16)
    velocity = jnp.dot(attended, w_out, preferred_element_type=jnp.float32) + jnp.dot(low_out, b_out, preferred_element_type=jnp.float32)
    denoised = (mixed_in - noise_level * velocity).astype(jnp.bfloat16)
    patch_pre = jnp.dot(denoised, w_patch, preferred_element_type=jnp.float32)
    return (low_out, patch_pre, lax.optimization_barrier(jnp.sum(jax.nn.gelu(patch_pre), axis=0)))

def reward(pooled, prompt):
    return logit_scale * jnp.sum(pooled * prompt) * lax.rsqrt(jnp.sum(pooled * pooled) + epsilon) * lax.rsqrt(jnp.sum(prompt * prompt) + epsilon)

def backward_out(patch_pre, grad_pooled, noise_level, attended, low_out, w_out, a_out, b_out, w_patch):
    gelu_back = jax.vjp(jax.nn.gelu, patch_pre)[1]
    grad_pre = gelu_back(jnp.broadcast_to(grad_pooled, patch_pre.shape))[0].astype(jnp.bfloat16)
    grad_denoised = lax.dot_general(grad_pre, w_patch, contract_last, preferred_element_type=jnp.float32)
    grad_velocity = (-noise_level * grad_denoised).astype(jnp.bfloat16)
    grad_low_out = lax.dot_general(grad_velocity, b_out, contract_last, preferred_element_type=jnp.float32).astype(jnp.bfloat16)
    grad_attended = (lax.dot_general(grad_velocity, w_out, contract_last, preferred_element_type=jnp.float32) + lax.dot_general(grad_low_out, a_out, contract_last, preferred_element_type=jnp.float32)).astype(jnp.bfloat16)
    grad_a_out = lax.dot_general(attended, grad_low_out, contract_first, preferred_element_type=jnp.float32)
    grad_b_out = lax.dot_general(low_out, grad_velocity, contract_first, preferred_element_type=jnp.float32)
    return (grad_denoised, grad_attended, grad_a_out, grad_b_out)

def backward_in(mixed_in, normed, low_rank, joined_qkv, grad_stacked, noise_level, w_qkv, a_qkv, b_qkv, qk_gain, head_size, grad_denoised):
    inner_width = joined_qkv.shape[1] // 3
    query_back = jax.vjp(lambda section: head_norm(section, qk_gain[0], head_size), joined_qkv[:, :inner_width])[1]
    key_back = jax.vjp(lambda section: head_norm(section, qk_gain[1], head_size), joined_qkv[:, inner_width:2 * inner_width])[1]
    grad_joined = jnp.concatenate([query_back(grad_stacked[:, 0].astype(jnp.float32))[0], key_back(grad_stacked[:, 1].astype(jnp.float32))[0], grad_stacked[:, 2].astype(jnp.float32)], axis=1).astype(jnp.bfloat16)
    grad_low = lax.dot_general(grad_joined, b_qkv, contract_last, preferred_element_type=jnp.float32).astype(jnp.bfloat16)
    grad_normed = lax.dot_general(grad_joined, w_qkv, contract_last, preferred_element_type=jnp.float32) + lax.dot_general(grad_low, a_qkv, contract_last, preferred_element_type=jnp.float32)
    grad_mixed = jax.vjp(layer_norm, mixed_in)[1](grad_normed)[0] + grad_denoised
    grad_latent = (1.0 - noise_level) * grad_mixed
    grad_a_qkv = lax.dot_general(normed, grad_low, contract_first, preferred_element_type=jnp.float32)
    grad_b_qkv = lax.dot_general(low_rank, grad_joined, contract_first, preferred_element_type=jnp.float32)
    return (grad_latent, grad_a_qkv, grad_b_qkv)

def reference(latent, noise, timestep, text_kv, qk_gain, prompt, w_qkv, a_qkv, b_qkv, w_out, a_out, b_out, w_patch):
    text_keys = head_norm(text_kv[0].astype(jnp.float32), qk_gain[1], HEAD_DIM).astype(jnp.bfloat16)
    text_values = text_kv[1]

    def replica(running, inputs):
        noise_rows, step_index = inputs
        noise_level = step_index.astype(jnp.float32) / 1000.0
        mixed_in, normed, low_rank, joined_qkv, stacked = project_in(latent, noise_rows, noise_level, w_qkv, a_qkv, b_qkv, qk_gain, HEAD_DIM)
        attended = attend(stacked, text_keys, text_values, HEAD_DIM)
        low_out, patch_pre, summed = project_out(attended, mixed_in, noise_level, w_out, a_out, b_out, w_patch)
        pooled = summed / TOKENS
        score_value, grad_pooled = jax.value_and_grad(reward)(pooled, prompt)
        grad_denoised, grad_attended, grad_a_out, grad_b_out = backward_out(patch_pre, grad_pooled, noise_level, attended, low_out, w_out, a_out, b_out, w_patch)
        grad_stacked = attend_back(stacked, text_keys, text_values, grad_attended, HEAD_DIM)
        grad_latent, grad_a_qkv, grad_b_qkv = backward_in(mixed_in, normed, low_rank, joined_qkv, grad_stacked, noise_level, w_qkv, a_qkv, b_qkv, qk_gain, HEAD_DIM, grad_denoised)
        updated = (running[0] + grad_latent, running[1] + grad_a_qkv, running[2] + grad_b_qkv, running[3] + grad_a_out, running[4] + grad_b_out)
        return (updated, score_value)
    initial = (jnp.zeros((TOKENS, D), jnp.float32), jnp.zeros((D, RANK), jnp.float32), jnp.zeros((RANK, 3 * HD), jnp.float32), jnp.zeros((HD, RANK), jnp.float32), jnp.zeros((RANK, D), jnp.float32))
    totals, rewards = lax.scan(replica, initial, (noise, timestep))
    return (rewards, totals[0], totals[1], totals[2], totals[3], totals[4])
```

```python
import functools

import jax
import jax.numpy as jnp
from jax import lax
from jax.experimental import pallas as pl
from jax.experimental.pallas import tpu as pltpu
from jax.sharding import PartitionSpec as P

HEAD_DIM = 64


epsilon = 1e-06
logit_scale = 100.0
contract_last = (((1,), (1,)), ((), ()))
contract_first = (((0,), (0,)), ((), ()))


def project_out(attended, mixed_in, noise_level, w_out, a_out, b_out, w_patch):
    low_out = jnp.dot(attended, a_out, preferred_element_type=jnp.float32).astype(jnp.bfloat16)
    velocity = jnp.dot(attended, w_out, preferred_element_type=jnp.float32) + jnp.dot(
        low_out, b_out, preferred_element_type=jnp.float32
    )
    denoised = (mixed_in - noise_level * velocity).astype(jnp.bfloat16)
    patch_pre = jnp.dot(denoised, w_patch, preferred_element_type=jnp.float32)
    return (low_out, patch_pre, jnp.sum(jax.nn.gelu(patch_pre), axis=0))


def reward(pooled, prompt):
    return (
        logit_scale
        * jnp.sum(pooled * prompt)
        * lax.rsqrt(jnp.sum(pooled * pooled) + epsilon)
        * lax.rsqrt(jnp.sum(prompt * prompt) + epsilon)
    )


def backward_out(
    patch_pre, grad_pooled, noise_level, attended, low_out, w_out, a_out, b_out, w_patch
):
    gelu_back = jax.vjp(jax.nn.gelu, patch_pre)[1]
    grad_pre = gelu_back(jnp.broadcast_to(grad_pooled, patch_pre.shape))[0].astype(jnp.bfloat16)
    grad_denoised = lax.dot_general(
        grad_pre, w_patch, contract_last, preferred_element_type=jnp.float32
    )
    grad_velocity = (-noise_level * grad_denoised).astype(jnp.bfloat16)
    grad_low_out = lax.dot_general(
        grad_velocity, b_out, contract_last, preferred_element_type=jnp.float32
    ).astype(jnp.bfloat16)
    grad_attended = (
        lax.dot_general(grad_velocity, w_out, contract_last, preferred_element_type=jnp.float32)
        + lax.dot_general(grad_low_out, a_out, contract_last, preferred_element_type=jnp.float32)
    ).astype(jnp.bfloat16)
    grad_a_out = lax.dot_general(
        attended, grad_low_out, contract_first, preferred_element_type=jnp.float32
    )
    grad_b_out = lax.dot_general(
        grad_velocity, low_out, contract_first, preferred_element_type=jnp.float32
    )
    return (grad_denoised, grad_attended, grad_a_out, grad_b_out)


MESH = pl.DeviceIdType.MESH
VMEM_LIMIT = 56 * 1024 * 1024
SCALE = HEAD_DIM**-0.5


def normalize(x, gain):
    return x * lax.rsqrt(jnp.mean(x * x, axis=-1, keepdims=True) + epsilon) * gain


def per_head(width):
    return [slice(at, at + HEAD_DIM) for at in range(0, width, HEAD_DIM)]


def attend_kernel(joined_ref, text_ref, gain_ref, att_ref, q_ref, k_ref, v_ref, inv_ref, vt, att_t):
    tokens, width = att_ref.shape
    text = text_ref.shape[1]
    chunk = inv_ref.shape[2]
    gain_q, gain_k = gain_ref[0:1], gain_ref[1:2]
    k_ref[pl.ds(tokens, text), :] = jnp.concatenate(
        [normalize(text_ref[0, :, h].astype(jnp.float32), gain_k) for h in per_head(width)], axis=1
    ).astype(jnp.bfloat16)
    v_ref[pl.ds(tokens, text), :] = text_ref[1]

    @pl.loop(0, tokens // chunk)
    def _(step):
        rows = pl.ds(pl.multiple_of(step * chunk, chunk), chunk)
        part = joined_ref[rows, :]
        q_ref[rows, :] = (
            jnp.concatenate(
                [normalize(part[:, h], gain_q) for h in per_head(width)], axis=1
            ).astype(jnp.bfloat16)
            * SCALE
        ).astype(jnp.bfloat16)
        k_ref[rows, :] = jnp.concatenate(
            [normalize(part[:, width : 2 * width][:, h], gain_k) for h in per_head(width)], axis=1
        ).astype(jnp.bfloat16)
        v_ref[rows, :] = part[:, 2 * width :].astype(jnp.bfloat16)

    vt[...] = v_ref[...].astype(jnp.float32).T.astype(jnp.bfloat16)

    @pl.loop(0, tokens // chunk)
    def _(step):
        rows = pl.ds(pl.multiple_of(step * chunk, chunk), chunk)
        for number, h in enumerate(per_head(width)):
            scores = lax.dot_general(
                k_ref[:, h], q_ref[rows, h], contract_last, preferred_element_type=jnp.float32
            )
            expped = jnp.exp(scores)
            inverse = 1.0 / jnp.sum(expped, axis=0, keepdims=True)
            inv_ref[step, pl.ds(number, 1), :] = inverse
            probs = (expped * inverse).astype(jnp.bfloat16)
            att_t[h, :] = jnp.dot(vt[h, :], probs, preferred_element_type=jnp.float32)
        att_ref[rows, :] = att_t[...].T.astype(jnp.bfloat16)


def attend(joined, text_kv, qk_gain):
    tokens, width = joined.shape[0], joined.shape[1] // 3
    text = text_kv.shape[1]
    chunk = 256 if tokens % 256 == 0 else tokens
    keys = tokens + text
    bf16 = jnp.bfloat16
    whole = pl.BlockSpec(memory_space=pltpu.VMEM)
    return pl.pallas_call(
        attend_kernel,
        out_shape=(
            jax.ShapeDtypeStruct((tokens, width), bf16),
            jax.ShapeDtypeStruct((tokens, width), bf16),
            jax.ShapeDtypeStruct((keys, width), bf16),
            jax.ShapeDtypeStruct((keys, width), bf16),
            jax.ShapeDtypeStruct((tokens // chunk, width // HEAD_DIM, chunk), jnp.float32),
        ),
        in_specs=[whole] * 3,
        out_specs=(whole,) * 5,
        scratch_shapes=[pltpu.VMEM((width, keys), bf16), pltpu.VMEM((width, chunk), jnp.float32)],
        compiler_params=pltpu.CompilerParams(vmem_limit_bytes=VMEM_LIMIT),
        name="attend",
    )(joined, text_kv, qk_gain)


def norm_back(x, gain, grad):
    rounded = grad.astype(jnp.bfloat16).astype(jnp.float32) * gain
    scale = lax.rsqrt(jnp.mean(x * x, axis=-1, keepdims=True) + epsilon)
    along = jnp.mean(rounded * x, axis=-1, keepdims=True)
    return scale * (rounded - x * (scale * scale * along))


def attend_back_kernel(
    joined_ref, q_ref, k_ref, v_ref, inv_ref, g_ref, gain_ref, out_ref, kt, grad_k, grad_v, grad_q
):
    tokens, width = q_ref.shape
    chunk = inv_ref.shape[2]
    gain_q, gain_k = gain_ref[0:1], gain_ref[1:2]
    kt[...] = k_ref[...].astype(jnp.float32).T.astype(jnp.bfloat16)
    grad_k[...] = jnp.zeros_like(grad_k)
    grad_v[...] = jnp.zeros_like(grad_v)

    @pl.loop(0, tokens // chunk)
    def _(step):
        rows = pl.ds(pl.multiple_of(step * chunk, chunk), chunk)
        for number, h in enumerate(per_head(width)):
            query, grad = q_ref[rows, h], g_ref[rows, h]
            scores = lax.dot_general(
                k_ref[:, h], query, contract_last, preferred_element_type=jnp.float32
            )
            probs = jnp.exp(scores) * inv_ref[step, pl.ds(number, 1), :]
            grad_probs = lax.dot_general(
                v_ref[:, h], grad, contract_last, preferred_element_type=jnp.float32
            )
            centre = jnp.sum(probs * grad_probs, axis=0, keepdims=True)
            grad_logits = (probs * (grad_probs - centre)).astype(jnp.bfloat16)
            grad_v[:, h] += jnp.dot(
                probs[:tokens].astype(jnp.bfloat16), grad, preferred_element_type=jnp.float32
            )
            grad_k[:, h] += jnp.dot(
                grad_logits[:tokens], query, preferred_element_type=jnp.float32
            )
            grad_q[h, :] = jnp.dot(kt[h, :], grad_logits, preferred_element_type=jnp.float32)
        back = grad_q[...].T * SCALE
        out_ref[rows, :width] = jnp.concatenate(
            [norm_back(joined_ref[rows, h], gain_q, back[:, h]) for h in per_head(width)], axis=1
        ).astype(jnp.bfloat16)

    @pl.loop(0, tokens // chunk)
    def _(step):
        rows = pl.ds(pl.multiple_of(step * chunk, chunk), chunk)
        part = joined_ref[rows, width : 2 * width]
        back = grad_k[rows, :]
        out_ref[rows, width : 2 * width] = jnp.concatenate(
            [norm_back(part[:, h], gain_k, back[:, h]) for h in per_head(width)], axis=1
        ).astype(jnp.bfloat16)
        out_ref[rows, 2 * width :] = grad_v[rows, :].astype(jnp.bfloat16)


def attend_back(joined, q, k, v, inverse, grad_heads, qk_gain):
    tokens, width = q.shape
    chunk = inverse.shape[2]
    whole = pl.BlockSpec(memory_space=pltpu.VMEM)
    return pl.pallas_call(
        attend_back_kernel,
        out_shape=jax.ShapeDtypeStruct((tokens, 3 * width), jnp.bfloat16),
        in_specs=[whole] * 7,
        out_specs=whole,
        scratch_shapes=[
            pltpu.VMEM((width, k.shape[0]), jnp.bfloat16),
            pltpu.VMEM((tokens, width), jnp.float32),
            pltpu.VMEM((tokens, width), jnp.float32),
            pltpu.VMEM((width, chunk), jnp.float32),
        ],
        compiler_params=pltpu.CompilerParams(vmem_limit_bytes=VMEM_LIMIT),
        name="attend_back",
    )(joined, q, k, v, inverse, grad_heads, qk_gain)


def reduce_kernel(
    sizes, lat_ref, ada_ref, lat_out, ada_out,
    pair_lat, pair_ada, sum_lat, sum_ada, seq_lat, seq_ada, tot_lat, tot_ada,
    part_lat, part_ada, rep_lat, rep_ada, gathered,
    pair_sems, seq_sems, rep_sems, last_sems,
):
    seqs, chips = sizes
    s, r = lax.axis_index("seq"), lax.axis_index("rep")
    z, c = r // 2, lax.rem(r, 2)
    other = 1 - c
    sibling = {"rep": 2 * z + other}
    seq_peers = [lax.rem(s + k, seqs) for k in range(seqs)]
    rep_peers = [lax.rem(z + k, chips) for k in range(chips)]

    barrier = pltpu.get_barrier_semaphore()
    peers = (
        [sibling]
        + [{"seq": p} for p in seq_peers[1:]]
        + [{"rep": 2 * p + c} for p in rep_peers[1:]]
    )
    for peer in peers:
        pl.semaphore_signal(barrier, inc=1, device_id=peer, device_id_type=MESH)
    pl.semaphore_wait(barrier, len(peers))

    def send(source, target, sems, index, peer):
        copy = pltpu.make_async_remote_copy(
            src_ref=source, dst_ref=target, send_sem=sems.at[0, index], recv_sem=sems.at[1, index],
            device_id=peer, device_id_type=MESH,
        )
        copy.start()
        return copy

    order = list(range(1, seqs)) + [0]
    pair_copies = {}
    for k in order:
        to = seq_peers[k]
        pair_copies[k] = (
            send(lat_ref.at[other, to], pair_lat.at[k], pair_sems, 2 * k, sibling),
            send(ada_ref.at[other, to], pair_ada.at[k], pair_sems, 2 * k + 1, sibling),
        )
    f32, bf16 = jnp.float32, jnp.bfloat16
    seq_copies = []
    for k in order:
        to = seq_peers[k]
        for copy in pair_copies[k]:
            copy.wait_recv()
        if k:
            for i in range(chips):
                sum_lat[k - 1, i] = (
                    lat_ref[c, to, i].astype(f32) + pair_lat[k, i].astype(f32)
                ).astype(bf16)
                sum_ada[k - 1, i] = (
                    ada_ref[c, to, i].astype(f32) + pair_ada[k, i].astype(f32)
                ).astype(bf16)
            seq_copies.append(
                send(sum_lat.at[k - 1], seq_lat.at[k - 1], seq_sems, 2 * k - 2, {"seq": to})
            )
            seq_copies.append(
                send(sum_ada.at[k - 1], seq_ada.at[k - 1], seq_sems, 2 * k - 1, {"seq": to})
            )
        else:
            for i in range(chips):
                tot_lat[i] = lat_ref[c, to, i].astype(f32) + pair_lat[k, i].astype(f32)
                tot_ada[i] = ada_ref[c, to, i].astype(f32) + pair_ada[k, i].astype(f32)
    for copy in seq_copies:
        copy.wait_recv()
    rep_copies = []
    for j in list(range(1, chips)) + [0]:
        to = rep_peers[j]
        lat, ada = tot_lat[to], tot_ada[to]
        for k in range(seqs - 1):
            lat += seq_lat[k, to].astype(f32)
            ada += seq_ada[k, to].astype(f32)
        if j:
            part_lat[j - 1] = lat.astype(bf16)
            part_ada[j - 1] = ada.astype(bf16)
            peer = {"rep": 2 * to + c}
            rep_copies.append(
                send(part_ada.at[j - 1], rep_ada.at[j - 1], rep_sems, 2 * j - 1, peer)
            )
            rep_copies.append(
                send(part_lat.at[j - 1], rep_lat.at[j - 1], rep_sems, 2 * j - 2, peer)
            )
        else:
            lat_out[...] = lat
            tot_ada[0] = ada
    for copy in rep_copies:
        copy.wait_recv()
    ada = tot_ada[0]
    for j in range(chips - 1):
        ada += rep_ada[j].astype(f32)
    gathered[s] = ada.astype(bf16)
    last_copies = []
    for k in range(1, seqs):
        last_copies.append(
            send(gathered.at[s], gathered.at[s], last_sems, k - 1, {"seq": seq_peers[k]})
        )
    lat = lat_out[...]
    for j in range(chips - 1):
        lat += rep_lat[j].astype(f32)
    lat_out[...] = lat
    for k in range(1, seqs):
        source = lax.rem(s - k + seqs, seqs)
        pltpu.make_async_remote_copy(
            src_ref=gathered.at[s], dst_ref=gathered.at[source], send_sem=last_sems.at[0, k - 1],
            recv_sem=last_sems.at[1, k - 1], device_id={"seq": source}, device_id_type=MESH,
        ).wait_recv()
    ada_out[...] = gathered[...].astype(f32)
    for copy in [one for pair in pair_copies.values() for one in pair] + seq_copies + rep_copies + last_copies:
        copy.wait_send()


def reduce_all(lat, ada):
    _, seqs, chips, rows, width = lat.shape
    a_rows, lanes = ada.shape[3:]
    bf16, f32 = jnp.bfloat16, jnp.float32
    whole = pl.BlockSpec(memory_space=pltpu.VMEM)

    def both(lead, kind=bf16):
        return [pltpu.VMEM(lead + (rows, width), kind), pltpu.VMEM(lead + (a_rows, lanes), kind)]

    sems = lambda count: pltpu.SemaphoreType.DMA((2, count))
    return pl.pallas_call(
        functools.partial(reduce_kernel, (seqs, chips)),
        out_shape=(
            jax.ShapeDtypeStruct((rows, width), f32),
            jax.ShapeDtypeStruct((seqs, a_rows, lanes), f32),
        ),
        in_specs=[whole] * 2,
        out_specs=(whole,) * 2,
        scratch_shapes=both((seqs, chips)) + both((seqs - 1, chips)) + both((seqs - 1, chips))
        + both((chips,), f32) + both((chips - 1,)) + both((chips - 1,))
        + [pltpu.VMEM((seqs, a_rows, lanes), bf16)]
        + [sems(2 * seqs), sems(2 * seqs - 2), sems(2 * chips - 2), sems(seqs - 1)],
        compiler_params=pltpu.CompilerParams(
            collective_id=0, has_side_effects=True, vmem_limit_bytes=VMEM_LIMIT
        ),
        name="reduce_all",
    )(lat, ada)


def shards(
    latent, noise, timestep, text_kv, qk_gain, prompt,
    w_qkv, a_qkv, b_qkv, w_out, a_out, b_out, w_patch,
):
    seqs, reps = lax.axis_size("seq"), lax.axis_size("rep")
    chips = reps // 2
    s = lax.axis_index("seq")
    bf16, f32 = jnp.bfloat16, jnp.float32
    rank = a_qkv.shape[1]
    inner = w_qkv.shape[1] // 3
    width = inner // seqs

    def my_columns(weight):
        parts = weight.reshape(weight.shape[0], 3, inner)
        return lax.dynamic_slice_in_dim(parts, s * width, width, 2).reshape(-1, 3 * width)

    w_in = lax.all_gather(my_columns(w_qkv), "rep", axis=0, tiled=True)
    b_in = my_columns(b_qkv)
    latent_rows = lax.all_gather(latent, "rep", axis=0, tiled=True)
    noise_level = timestep[0].astype(f32) / 1000.0
    mixed_in = (1.0 - noise_level) * latent_rows.astype(f32) + noise_level * noise[0].astype(f32)
    centred = mixed_in - jnp.mean(mixed_in, axis=-1, keepdims=True)
    deviation = lax.rsqrt(jnp.mean(centred * centred, axis=-1, keepdims=True) + epsilon)
    normed = lax.all_gather((centred * deviation).astype(bf16), "seq", axis=0, tiled=True)
    deviation = lax.all_gather(deviation, "seq", axis=0, tiled=True)
    w_in, normed, w_out = lax.optimization_barrier((w_in, normed, w_out))
    w_back = lax.all_gather(w_out, "rep", axis=0, tiled=True)

    low_rank = jnp.dot(normed, a_qkv, preferred_element_type=f32).astype(bf16)
    joined = jnp.dot(normed, w_in, preferred_element_type=f32) + jnp.dot(
        low_rank, b_in, preferred_element_type=f32
    )
    attended_heads, q, k, v, inverse = attend(joined, text_kv, qk_gain)
    attended = lax.all_to_all(attended_heads, "seq", split_axis=0, concat_axis=1, tiled=True)
    low_out, patch_pre, partial_sum = project_out(
        attended, mixed_in, noise_level, w_back, a_out, b_out, w_patch
    )
    pooled = lax.psum(partial_sum, "seq") / (latent_rows.shape[0] * seqs)
    score_value, grad_pooled = jax.value_and_grad(reward)(pooled, prompt)
    grad_denoised, grad_attended, grad_a_out, grad_b_out = backward_out(
        patch_pre, grad_pooled, noise_level, attended, low_out, w_back, a_out, b_out, w_patch
    )
    grad_heads = lax.all_to_all(grad_attended, "seq", split_axis=1, concat_axis=0, tiled=True)
    grad_joined = attend_back(joined, q, k, v, inverse, grad_heads, qk_gain)

    grad_low = lax.dot_general(
        grad_joined, b_in, contract_last, preferred_element_type=f32
    ).astype(bf16)
    grad_normed = lax.dot_general(
        grad_joined, w_in, contract_last, preferred_element_type=f32
    ) + lax.dot_general(grad_low, a_qkv, contract_last, preferred_element_type=f32)
    normed32 = normed.astype(f32)
    grad_mixed = deviation * (
        grad_normed
        - jnp.mean(grad_normed, axis=-1, keepdims=True)
        - normed32 * jnp.mean(grad_normed * normed32, axis=-1, keepdims=True)
    )
    tokens, model = grad_mixed.shape
    rows = tokens // seqs
    mine = (lax.broadcasted_iota(jnp.int32, (seqs, 1, 1), 0) == s).astype(f32)
    grad_mixed = grad_mixed.reshape(seqs, rows, model) + mine * grad_denoised[None]
    lat = ((1.0 - noise_level) * grad_mixed).astype(bf16)
    lat = lat.reshape(seqs, chips, 2, rows // reps, model).transpose(2, 0, 1, 3, 4)

    grad_a_qkv = lax.dot_general(normed, grad_low, contract_first, preferred_element_type=f32)
    grad_b_qkv = lax.dot_general(grad_joined, low_rank, contract_first, preferred_element_type=f32)
    spread = jnp.zeros((3, seqs, width, rank), bf16)
    spread = lax.dynamic_update_slice(
        spread, grad_b_qkv.astype(bf16).reshape(3, 1, width, rank), (0, s, 0, 0)
    )
    by_rep = [
        grad_a_qkv.astype(bf16).reshape(reps, -1, rank),
        spread.reshape(reps, -1, rank),
        grad_a_out.astype(bf16).reshape(reps, -1, rank),
        grad_b_out.astype(bf16).reshape(reps, -1, rank),
    ]
    lengths = [one.shape[1] for one in by_rep]
    ada = jnp.concatenate(by_rep, axis=1)
    half = ada.shape[1] // 2
    ada = jnp.concatenate([ada[:, :half], ada[:, half:]], axis=2)
    ada = ada.reshape(chips, 2, seqs, half // seqs, 2 * rank).transpose(1, 2, 0, 3, 4)
    latent_grad, ada = reduce_all(lat, ada)
    ada = ada.reshape(half, 2 * rank)
    ada = jnp.concatenate([ada[:, :rank], ada[:, rank:]], axis=0)
    pieces, at = [], 0
    for length in lengths:
        pieces.append(ada[at : at + length])
        at += length
    return (
        score_value.reshape(1), latent_grad, pieces[0], pieces[1].T, pieces[2], pieces[3].T,
    )


def solution(mesh):
    in_specs = (
        P(("seq", "rep"), None),
        P("rep", "seq", None),
        P("rep"),
        P(None, None, "seq"),
        P(),
        P(),
        P("rep", None),
        P(),
        P(),
        P("rep", None),
        P(),
        P(),
        P(),
    )
    out_specs = (
        P("rep"),
        P(("seq", "rep"), None),
        P("rep", None),
        P(None, "rep"),
        P("rep", None),
        P(None, "rep"),
    )
    return jax.shard_map(shards, mesh=mesh, in_specs=in_specs, out_specs=out_specs, check_vma=False)
```

```python
import functools

import jax
import jax.numpy as jnp
from jax import lax
from jax.experimental import pallas as pl
from jax.experimental.pallas import tpu as pltpu
from jax.sharding import PartitionSpec as P

HEAD_DIM = 64


epsilon = 1e-06
logit_scale = 100.0
contract_last = (((1,), (1,)), ((), ()))
contract_first = (((0,), (0,)), ((), ()))


def project_out(attended, mixed_in, noise_level, w_out, a_out, b_out, w_patch):
    low_out = jnp.dot(attended, a_out, preferred_element_type=jnp.float32).astype(jnp.bfloat16)
    velocity = jnp.dot(attended, w_out, preferred_element_type=jnp.float32) + jnp.dot(
        low_out, b_out, preferred_element_type=jnp.float32
    )
    denoised = (mixed_in - noise_level * velocity).astype(jnp.bfloat16)
    patch_pre = jnp.dot(denoised, w_patch, preferred_element_type=jnp.float32)
    return (low_out, patch_pre, jnp.sum(jax.nn.gelu(patch_pre), axis=0))


def reward(pooled, prompt):
    return (
        logit_scale
        * jnp.sum(pooled * prompt)
        * lax.rsqrt(jnp.sum(pooled * pooled) + epsilon)
        * lax.rsqrt(jnp.sum(prompt * prompt) + epsilon)
    )


def backward_out(
    patch_pre, grad_pooled, noise_level, attended, low_out, w_out, a_out, b_out, w_patch
):
    gelu_back = jax.vjp(jax.nn.gelu, patch_pre)[1]
    grad_pre = gelu_back(jnp.broadcast_to(grad_pooled, patch_pre.shape))[0].astype(jnp.bfloat16)
    grad_denoised = lax.dot_general(
        grad_pre, w_patch, contract_last, preferred_element_type=jnp.float32
    )
    grad_velocity = (-noise_level * grad_denoised).astype(jnp.bfloat16)
    grad_low_out = lax.dot_general(
        grad_velocity, b_out, contract_last, preferred_element_type=jnp.float32
    ).astype(jnp.bfloat16)
    grad_attended = (
        lax.dot_general(grad_velocity, w_out, contract_last, preferred_element_type=jnp.float32)
        + lax.dot_general(grad_low_out, a_out, contract_last, preferred_element_type=jnp.float32)
    ).astype(jnp.bfloat16)
    grad_a_out = lax.dot_general(
        attended, grad_low_out, contract_first, preferred_element_type=jnp.float32
    )
    grad_b_out = lax.dot_general(
        grad_velocity, low_out, contract_first, preferred_element_type=jnp.float32
    )
    return (grad_denoised, grad_attended, grad_a_out, grad_b_out)


MESH = pl.DeviceIdType.MESH
VMEM_LIMIT = 56 * 1024 * 1024
SCALE = HEAD_DIM**-0.5


def normalize(x, gain):
    return x * lax.rsqrt(jnp.mean(x * x, axis=-1, keepdims=True) + epsilon) * gain


def per_head(width):
    return [slice(at, at + HEAD_DIM) for at in range(0, width, HEAD_DIM)]


def attend_kernel(joined_ref, text_ref, gain_ref, att_ref, q_ref, k_ref, v_ref, inv_ref, vt, att_t):
    tokens, width = att_ref.shape
    text = text_ref.shape[1]
    chunk = inv_ref.shape[2]
    gain_q, gain_k = gain_ref[0:1], gain_ref[1:2]
    k_ref[pl.ds(tokens, text), :] = jnp.concatenate(
        [normalize(text_ref[0, :, h].astype(jnp.float32), gain_k) for h in per_head(width)], axis=1
    ).astype(jnp.bfloat16)
    v_ref[pl.ds(tokens, text), :] = text_ref[1]

    @pl.loop(0, tokens // chunk)
    def _(step):
        rows = pl.ds(pl.multiple_of(step * chunk, chunk), chunk)
        part = joined_ref[rows, :]
        q_ref[rows, :] = (
            jnp.concatenate(
                [normalize(part[:, h], gain_q) for h in per_head(width)], axis=1
            ).astype(jnp.bfloat16)
            * SCALE
        ).astype(jnp.bfloat16)
        k_ref[rows, :] = jnp.concatenate(
            [normalize(part[:, width : 2 * width][:, h], gain_k) for h in per_head(width)], axis=1
        ).astype(jnp.bfloat16)
        v_ref[rows, :] = part[:, 2 * width :].astype(jnp.bfloat16)

    vt[...] = v_ref[...].astype(jnp.float32).T.astype(jnp.bfloat16)

    @pl.loop(0, tokens // chunk)
    def _(step):
        rows = pl.ds(pl.multiple_of(step * chunk, chunk), chunk)
        for number, h in enumerate(per_head(width)):
            scores = lax.dot_general(
                k_ref[:, h], q_ref[rows, h], contract_last, preferred_element_type=jnp.float32
            )
            expped = jnp.exp(scores)
            inverse = 1.0 / jnp.sum(expped, axis=0, keepdims=True)
            inv_ref[step, pl.ds(number, 1), :] = inverse
            probs = (expped * inverse).astype(jnp.bfloat16)
            att_t[h, :] = jnp.dot(vt[h, :], probs, preferred_element_type=jnp.float32)
        att_ref[rows, :] = att_t[...].T.astype(jnp.bfloat16)


def attend(joined, text_kv, qk_gain):
    tokens, width = joined.shape[0], joined.shape[1] // 3
    text = text_kv.shape[1]
    chunk = 256 if tokens % 256 == 0 else tokens
    keys = tokens + text
    bf16 = jnp.bfloat16
    whole = pl.BlockSpec(memory_space=pltpu.VMEM)
    return pl.pallas_call(
        attend_kernel,
        out_shape=(
            jax.ShapeDtypeStruct((tokens, width), bf16),
            jax.ShapeDtypeStruct((tokens, width), bf16),
            jax.ShapeDtypeStruct((keys, width), bf16),
            jax.ShapeDtypeStruct((keys, width), bf16),
            jax.ShapeDtypeStruct((tokens // chunk, width // HEAD_DIM, chunk), jnp.float32),
        ),
        in_specs=[whole] * 3,
        out_specs=(whole,) * 5,
        scratch_shapes=[pltpu.VMEM((width, keys), bf16), pltpu.VMEM((width, chunk), jnp.float32)],
        compiler_params=pltpu.CompilerParams(vmem_limit_bytes=VMEM_LIMIT),
        name="attend",
    )(joined, text_kv, qk_gain)


def norm_back(x, gain, grad):
    rounded = grad.astype(jnp.bfloat16).astype(jnp.float32) * gain
    scale = lax.rsqrt(jnp.mean(x * x, axis=-1, keepdims=True) + epsilon)
    along = jnp.mean(rounded * x, axis=-1, keepdims=True)
    return scale * (rounded - x * (scale * scale * along))


def attend_back_kernel(
    joined_ref, q_ref, k_ref, v_ref, inv_ref, g_ref, gain_ref, out_ref, kt, grad_k, grad_v, grad_q
):
    tokens, width = q_ref.shape
    chunk = inv_ref.shape[2]
    gain_q, gain_k = gain_ref[0:1], gain_ref[1:2]
    kt[...] = k_ref[...].astype(jnp.float32).T.astype(jnp.bfloat16)
    grad_k[...] = jnp.zeros_like(grad_k)
    grad_v[...] = jnp.zeros_like(grad_v)

    @pl.loop(0, tokens // chunk)
    def _(step):
        rows = pl.ds(pl.multiple_of(step * chunk, chunk), chunk)
        for number, h in enumerate(per_head(width)):
            query, grad = q_ref[rows, h], g_ref[rows, h]
            scores = lax.dot_general(
                k_ref[:, h], query, contract_last, preferred_element_type=jnp.float32
            )
            probs = jnp.exp(scores) * inv_ref[step, pl.ds(number, 1), :]
            grad_probs = lax.dot_general(
                v_ref[:, h], grad, contract_last, preferred_element_type=jnp.float32
            )
            centre = jnp.sum(probs * grad_probs, axis=0, keepdims=True)
            grad_logits = (probs * (grad_probs - centre)).astype(jnp.bfloat16)
            grad_v[:, h] += jnp.dot(
                probs[:tokens].astype(jnp.bfloat16), grad, preferred_element_type=jnp.float32
            )
            grad_k[:, h] += jnp.dot(
                grad_logits[:tokens], query, preferred_element_type=jnp.float32
            )
            grad_q[h, :] = jnp.dot(kt[h, :], grad_logits, preferred_element_type=jnp.float32)
        back = grad_q[...].T * SCALE
        out_ref[rows, :width] = jnp.concatenate(
            [norm_back(joined_ref[rows, h], gain_q, back[:, h]) for h in per_head(width)], axis=1
        ).astype(jnp.bfloat16)

    @pl.loop(0, tokens // chunk)
    def _(step):
        rows = pl.ds(pl.multiple_of(step * chunk, chunk), chunk)
        part = joined_ref[rows, width : 2 * width]
        back = grad_k[rows, :]
        out_ref[rows, width : 2 * width] = jnp.concatenate(
            [norm_back(part[:, h], gain_k, back[:, h]) for h in per_head(width)], axis=1
        ).astype(jnp.bfloat16)
        out_ref[rows, 2 * width :] = grad_v[rows, :].astype(jnp.bfloat16)


def attend_back(joined, q, k, v, inverse, grad_heads, qk_gain):
    tokens, width = q.shape
    chunk = inverse.shape[2]
    whole = pl.BlockSpec(memory_space=pltpu.VMEM)
    return pl.pallas_call(
        attend_back_kernel,
        out_shape=jax.ShapeDtypeStruct((tokens, 3 * width), jnp.bfloat16),
        in_specs=[whole] * 7,
        out_specs=whole,
        scratch_shapes=[
            pltpu.VMEM((width, k.shape[0]), jnp.bfloat16),
            pltpu.VMEM((tokens, width), jnp.float32),
            pltpu.VMEM((tokens, width), jnp.float32),
            pltpu.VMEM((width, chunk), jnp.float32),
        ],
        compiler_params=pltpu.CompilerParams(vmem_limit_bytes=VMEM_LIMIT),
        name="attend_back",
    )(joined, q, k, v, inverse, grad_heads, qk_gain)


def reduce_kernel(
    sizes, lat_ref, ada_ref, lat_out, ada_out,
    pair_lat, pair_ada, sum_lat, sum_ada, seq_lat, seq_ada, tot_lat, tot_ada,
    part_lat, part_ada, rep_lat, rep_ada, gathered,
    pair_sems, seq_sems, rep_sems, last_sems,
):
    seqs, chips = sizes
    s, r = lax.axis_index("seq"), lax.axis_index("rep")
    z, c = r // 2, lax.rem(r, 2)
    other = 1 - c
    sibling = {"rep": 2 * z + other}
    seq_peers = [lax.rem(s + k, seqs) for k in range(seqs)]
    rep_peers = [lax.rem(z + k, chips) for k in range(chips)]

    barrier = pltpu.get_barrier_semaphore()
    peers = (
        [sibling]
        + [{"seq": p} for p in seq_peers[1:]]
        + [{"rep": 2 * p + c} for p in rep_peers[1:]]
    )
    for peer in peers:
        pl.semaphore_signal(barrier, inc=1, device_id=peer, device_id_type=MESH)
    pl.semaphore_wait(barrier, len(peers))

    def send(source, target, sems, index, peer):
        copy = pltpu.make_async_remote_copy(
            src_ref=source, dst_ref=target, send_sem=sems.at[0, index], recv_sem=sems.at[1, index],
            device_id=peer, device_id_type=MESH,
        )
        copy.start()
        return copy

    order = list(range(1, seqs)) + [0]
    pair_copies = {}
    for k in order:
        to = seq_peers[k]
        pair_copies[k] = (
            send(lat_ref.at[other, to], pair_lat.at[k], pair_sems, 2 * k, sibling),
            send(ada_ref.at[other, to], pair_ada.at[k], pair_sems, 2 * k + 1, sibling),
        )
    f32, bf16 = jnp.float32, jnp.bfloat16
    seq_copies = []
    for k in order:
        to = seq_peers[k]
        for copy in pair_copies[k]:
            copy.wait_recv()
        if k:
            for i in range(chips):
                sum_lat[k - 1, i] = (
                    lat_ref[c, to, i].astype(f32) + pair_lat[k, i].astype(f32)
                ).astype(bf16)
                sum_ada[k - 1, i] = (
                    ada_ref[c, to, i].astype(f32) + pair_ada[k, i].astype(f32)
                ).astype(bf16)
            seq_copies.append(
                send(sum_lat.at[k - 1], seq_lat.at[k - 1], seq_sems, 2 * k - 2, {"seq": to})
            )
            seq_copies.append(
                send(sum_ada.at[k - 1], seq_ada.at[k - 1], seq_sems, 2 * k - 1, {"seq": to})
            )
        else:
            for i in range(chips):
                tot_lat[i] = lat_ref[c, to, i].astype(f32) + pair_lat[k, i].astype(f32)
                tot_ada[i] = ada_ref[c, to, i].astype(f32) + pair_ada[k, i].astype(f32)
    for copy in seq_copies:
        copy.wait_recv()
    rep_copies = []
    for j in list(range(1, chips)) + [0]:
        to = rep_peers[j]
        lat, ada = tot_lat[to], tot_ada[to]
        for k in range(seqs - 1):
            lat += seq_lat[k, to].astype(f32)
            ada += seq_ada[k, to].astype(f32)
        if j:
            part_lat[j - 1] = lat.astype(bf16)
            part_ada[j - 1] = ada.astype(bf16)
            peer = {"rep": 2 * to + c}
            rep_copies.append(
                send(part_ada.at[j - 1], rep_ada.at[j - 1], rep_sems, 2 * j - 1, peer)
            )
            rep_copies.append(
                send(part_lat.at[j - 1], rep_lat.at[j - 1], rep_sems, 2 * j - 2, peer)
            )
        else:
            lat_out[...] = lat
            tot_ada[0] = ada
    for copy in rep_copies:
        copy.wait_recv()
    ada = tot_ada[0]
    for j in range(chips - 1):
        ada += rep_ada[j].astype(f32)
    gathered[s] = ada.astype(bf16)
    last_copies = []
    for k in range(1, seqs):
        last_copies.append(
            send(gathered.at[s], gathered.at[s], last_sems, k - 1, {"seq": seq_peers[k]})
        )
    lat = lat_out[...]
    for j in range(chips - 1):
        lat += rep_lat[j].astype(f32)
    lat_out[...] = lat
    for k in range(1, seqs):
        source = lax.rem(s - k + seqs, seqs)
        pltpu.make_async_remote_copy(
            src_ref=gathered.at[s], dst_ref=gathered.at[source], send_sem=last_sems.at[0, k - 1],
            recv_sem=last_sems.at[1, k - 1], device_id={"seq": source}, device_id_type=MESH,
        ).wait_recv()
    ada_out[...] = gathered[...].astype(f32)
    for copy in [one for pair in pair_copies.values() for one in pair] + seq_copies + rep_copies + last_copies:
        copy.wait_send()


def reduce_all(lat, ada):
    _, seqs, chips, rows, width = lat.shape
    a_rows, lanes = ada.shape[3:]
    bf16, f32 = jnp.bfloat16, jnp.float32
    whole = pl.BlockSpec(memory_space=pltpu.VMEM)

    def both(lead, kind=bf16):
        return [pltpu.VMEM(lead + (rows, width), kind), pltpu.VMEM(lead + (a_rows, lanes), kind)]

    sems = lambda count: pltpu.SemaphoreType.DMA((2, count))
    return pl.pallas_call(
        functools.partial(reduce_kernel, (seqs, chips)),
        out_shape=(
            jax.ShapeDtypeStruct((rows, width), f32),
            jax.ShapeDtypeStruct((seqs, a_rows, lanes), f32),
        ),
        in_specs=[whole] * 2,
        out_specs=(whole,) * 2,
        scratch_shapes=both((seqs, chips)) + both((seqs - 1, chips)) + both((seqs - 1, chips))
        + both((chips,), f32) + both((chips - 1,)) + both((chips - 1,))
        + [pltpu.VMEM((seqs, a_rows, lanes), bf16)]
        + [sems(2 * seqs), sems(2 * seqs - 2), sems(2 * chips - 2), sems(seqs - 1)],
        compiler_params=pltpu.CompilerParams(
            collective_id=0, has_side_effects=True, vmem_limit_bytes=VMEM_LIMIT
        ),
        name="reduce_all",
    )(lat, ada)


def gather_kernel(
    sizes, level_ref, lat_ref, noise_ref, w_ref,
    w_out_ref, normed_ref, dev_ref, mixed_ref,
    lat_all, lat_rows, own_sem, lat_sems, w_sems, norm_sems, dev_sems,
):
    seqs, chips = sizes
    s, r = lax.axis_index("seq"), lax.axis_index("rep")
    z, c = r // 2, lax.rem(r, 2)
    sibling = {"rep": 2 * z + 1 - c}
    ahead = [lax.rem(z + j, chips) for j in range(chips)]
    behind = [lax.rem(z - j + chips, chips) for j in range(chips)]
    seq_ahead = [lax.rem(s + k, seqs) for k in range(seqs)]
    seq_behind = [lax.rem(s - k + seqs, seqs) for k in range(seqs)]
    f32, bf16 = jnp.float32, jnp.bfloat16

    barrier = pltpu.get_barrier_semaphore()
    peers = (
        [sibling]
        + [{"seq": p} for p in seq_ahead[1:]]
        + [{"rep": 2 * p + c} for p in ahead[1:]]
    )
    for peer in peers:
        pl.semaphore_signal(barrier, inc=1, device_id=peer, device_id_type=MESH)
    pl.semaphore_wait(barrier, len(peers))

    def copy(source, target, sems, index, peer):
        return pltpu.make_async_remote_copy(
            src_ref=source, dst_ref=target, send_sem=sems.at[0, index], recv_sem=sems.at[1, index],
            device_id=peer, device_id_type=MESH,
        )

    started = []

    def send(*args):
        one = copy(*args)
        one.start()
        started.append(one)

    for source, target, sems in ((lat_ref, lat_all, lat_sems), (w_ref, w_out_ref, w_sems)):
        for j in range(1, chips):
            send(source, target.at[r], sems, j, {"rep": 2 * ahead[j] + c})
        send(source, target.at[r], sems, chips, sibling)
    own = pltpu.make_async_copy(w_ref, w_out_ref.at[r], own_sem)
    own.start()
    lat_all[r] = lat_ref[...]

    def forward(target, sems):
        for j in range(1, chips):
            block = target.at[2 * behind[j] + c]
            copy(block, block, sems, j, sibling).wait_recv()
            send(block, block, sems, chips + j, sibling)

    def arrive(target, sems):
        for j in range(chips):
            block = target.at[2 * behind[j] + 1 - c]
            copy(block, block, sems, chips + j, sibling).wait_recv()

    forward(lat_all, lat_sems)
    arrive(lat_all, lat_sems)
    length = lat_ref.shape[0]
    rows = noise_ref.shape[0]
    for i in range(2 * chips):
        lat_rows[i * length : (i + 1) * length, :] = lat_all[i].astype(f32)
    level = level_ref[0:1, 0:1]
    chunk = 32 if rows % 32 == 0 else rows

    @pl.loop(0, rows // chunk)
    def _(step):
        at = pl.ds(pl.multiple_of(step * chunk, chunk), chunk)
        mixed = (1.0 - level) * lat_rows[at, :] + level * noise_ref[at, :].astype(f32)
        mixed_ref[at, :] = mixed
        centred = mixed - jnp.mean(mixed, axis=-1, keepdims=True)
        deviation = lax.rsqrt(jnp.mean(centred * centred, axis=-1, keepdims=True) + epsilon)
        normed_ref[s, at, :] = (centred * deviation).astype(bf16)
        dev_ref[s, at, :] = jnp.broadcast_to(deviation, (chunk, dev_ref.shape[2]))

    for k in range(1, seqs):
        send(normed_ref.at[s], normed_ref.at[s], norm_sems, k - 1, {"seq": seq_ahead[k]})
        send(dev_ref.at[s], dev_ref.at[s], dev_sems, k - 1, {"seq": seq_ahead[k]})
    forward(w_out_ref, w_sems)
    own.wait()
    for k in range(1, seqs):
        for target, sems in ((normed_ref, norm_sems), (dev_ref, dev_sems)):
            block = target.at[seq_behind[k]]
            copy(block, block, sems, k - 1, {"seq": seq_ahead[k]}).wait_recv()
    arrive(w_out_ref, w_sems)
    for one in started:
        one.wait_send()


def gather_all(level, latent, noise, weight):
    seqs, reps = lax.axis_size("seq"), lax.axis_size("rep")
    chips = reps // 2
    rows, model = noise.shape
    bf16, f32 = jnp.bfloat16, jnp.float32
    whole = pl.BlockSpec(memory_space=pltpu.VMEM)
    sems = lambda count: pltpu.SemaphoreType.DMA((2, count))
    return pl.pallas_call(
        functools.partial(gather_kernel, (seqs, chips)),
        out_shape=(
            jax.ShapeDtypeStruct((reps,) + weight.shape, bf16),
            jax.ShapeDtypeStruct((seqs, rows, model), bf16),
            jax.ShapeDtypeStruct((seqs, rows, 128), f32),
            jax.ShapeDtypeStruct((rows, model), f32),
        ),
        in_specs=[whole] * 4,
        out_specs=(whole,) * 4,
        scratch_shapes=[
            pltpu.VMEM((reps,) + latent.shape, bf16),
            pltpu.VMEM((rows, model), f32),
            pltpu.SemaphoreType.DMA,
            sems(2 * chips), sems(2 * chips), sems(seqs - 1), sems(seqs - 1),
        ],
        compiler_params=pltpu.CompilerParams(
            collective_id=1, has_side_effects=True, vmem_limit_bytes=VMEM_LIMIT
        ),
        cost_estimate=pl.CostEstimate(flops=10**10, bytes_accessed=2 * 10**8, transcendentals=0),
        name="gather_all",
    )(level, latent, noise, weight)


def shards(
    latent, noise, timestep, text_kv, qk_gain, prompt,
    w_qkv, a_qkv, b_qkv, w_out, a_out, b_out, w_patch,
):
    seqs, reps = lax.axis_size("seq"), lax.axis_size("rep")
    chips = reps // 2
    s = lax.axis_index("seq")
    bf16, f32 = jnp.bfloat16, jnp.float32
    rank = a_qkv.shape[1]
    inner = w_qkv.shape[1] // 3
    width = inner // seqs

    def my_columns(weight):
        return jnp.concatenate(
            [
                lax.dynamic_slice_in_dim(weight, part * inner + s * width, width, 1)
                for part in range(3)
            ],
            axis=1,
        )

    w_back = lax.all_gather(w_out, "rep", axis=0, tiled=True)
    b_in = my_columns(b_qkv)
    noise_level = timestep[0].astype(f32) / 1000.0
    w_in, normed, deviation, mixed_in = gather_all(
        jnp.full((1, 128), noise_level), latent, noise[0], my_columns(w_qkv)
    )
    w_in = w_in.reshape(-1, 3 * width)
    normed = normed.reshape(-1, normed.shape[2])
    deviation = deviation.reshape(-1, deviation.shape[2])[:, :1]

    low_rank = jnp.dot(normed, a_qkv, preferred_element_type=f32).astype(bf16)
    joined = jnp.dot(normed, w_in, preferred_element_type=f32) + jnp.dot(
        low_rank, b_in, preferred_element_type=f32
    )
    attended_heads, q, k, v, inverse = attend(joined, text_kv, qk_gain)
    attended = lax.all_to_all(attended_heads, "seq", split_axis=0, concat_axis=1, tiled=True)
    low_out, patch_pre, partial_sum = project_out(
        attended, mixed_in, noise_level, w_back, a_out, b_out, w_patch
    )
    pooled = lax.psum(partial_sum, "seq") / normed.shape[0]
    score_value, grad_pooled = jax.value_and_grad(reward)(pooled, prompt)
    grad_denoised, grad_attended, grad_a_out, grad_b_out = backward_out(
        patch_pre, grad_pooled, noise_level, attended, low_out, w_back, a_out, b_out, w_patch
    )
    grad_heads = lax.all_to_all(grad_attended, "seq", split_axis=1, concat_axis=0, tiled=True)
    grad_joined = attend_back(joined, q, k, v, inverse, grad_heads, qk_gain)

    grad_low = lax.dot_general(
        grad_joined, b_in, contract_last, preferred_element_type=f32
    ).astype(bf16)
    grad_normed = lax.dot_general(
        grad_joined, w_in, contract_last, preferred_element_type=f32
    ) + lax.dot_general(grad_low, a_qkv, contract_last, preferred_element_type=f32)
    normed32 = normed.astype(f32)
    grad_mixed = deviation * (
        grad_normed
        - jnp.mean(grad_normed, axis=-1, keepdims=True)
        - normed32 * jnp.mean(grad_normed * normed32, axis=-1, keepdims=True)
    )
    tokens, model = grad_mixed.shape
    rows = tokens // seqs
    mine = (lax.broadcasted_iota(jnp.int32, (seqs, 1, 1), 0) == s).astype(f32)
    grad_mixed = grad_mixed.reshape(seqs, rows, model) + mine * grad_denoised[None]
    lat = ((1.0 - noise_level) * grad_mixed).astype(bf16)
    lat = lat.reshape(seqs, chips, 2, rows // reps, model).transpose(2, 0, 1, 3, 4)

    grad_a_qkv = lax.dot_general(normed, grad_low, contract_first, preferred_element_type=f32)
    grad_b_qkv = lax.dot_general(grad_joined, low_rank, contract_first, preferred_element_type=f32)
    spread = jnp.zeros((3, seqs, width, rank), bf16)
    spread = lax.dynamic_update_slice(
        spread, grad_b_qkv.astype(bf16).reshape(3, 1, width, rank), (0, s, 0, 0)
    )
    by_rep = [
        grad_a_qkv.astype(bf16).reshape(reps, -1, rank),
        spread.reshape(reps, -1, rank),
        grad_a_out.astype(bf16).reshape(reps, -1, rank),
        grad_b_out.astype(bf16).reshape(reps, -1, rank),
    ]
    lengths = [one.shape[1] for one in by_rep]
    ada = jnp.concatenate(by_rep, axis=1)
    half = ada.shape[1] // 2
    ada = jnp.concatenate([ada[:, :half], ada[:, half:]], axis=2)
    ada = ada.reshape(chips, 2, seqs, half // seqs, 2 * rank).transpose(1, 2, 0, 3, 4)
    latent_grad, ada = reduce_all(lat, ada)
    ada = ada.reshape(half, 2 * rank)
    ada = jnp.concatenate([ada[:, :rank], ada[:, rank:]], axis=0)
    pieces, at = [], 0
    for length in lengths:
        pieces.append(ada[at : at + length])
        at += length
    return (
        score_value.reshape(1), latent_grad, pieces[0], pieces[1].T, pieces[2], pieces[3].T,
    )


def solution(mesh):
    in_specs = (
        P(("seq", "rep"), None),
        P("rep", "seq", None),
        P("rep"),
        P(None, None, "seq"),
        P(),
        P(),
        P("rep", None),
        P(),
        P(),
        P("rep", None),
        P(),
        P(),
        P(),
    )
    out_specs = (
        P("rep"),
        P(("seq", "rep"), None),
        P("rep", None),
        P(None, "rep"),
        P("rep", None),
        P(None, "rep"),
    )
    return jax.shard_map(shards, mesh=mesh, in_specs=in_specs, out_specs=out_specs, check_vma=False)
```

```python
import functools

import jax
import jax.numpy as jnp
from jax import lax
from jax.experimental import pallas as pl
from jax.experimental.pallas import tpu as pltpu
from jax.sharding import PartitionSpec as P

HEAD_DIM = 64


epsilon = 1e-06
logit_scale = 100.0
contract_last = (((1,), (1,)), ((), ()))
contract_first = (((0,), (0,)), ((), ()))


def project_out(attended, mixed_in, noise_level, w_out, a_out, b_out, w_patch):
    low_out = jnp.dot(attended, a_out, preferred_element_type=jnp.float32).astype(jnp.bfloat16)
    velocity = jnp.dot(attended, w_out, preferred_element_type=jnp.float32) + jnp.dot(
        low_out, b_out, preferred_element_type=jnp.float32
    )
    denoised = (mixed_in - noise_level * velocity).astype(jnp.bfloat16)
    patch_pre = jnp.dot(denoised, w_patch, preferred_element_type=jnp.float32)
    return (low_out, patch_pre, jnp.sum(jax.nn.gelu(patch_pre), axis=0))


def reward(pooled, prompt):
    return (
        logit_scale
        * jnp.sum(pooled * prompt)
        * lax.rsqrt(jnp.sum(pooled * pooled) + epsilon)
        * lax.rsqrt(jnp.sum(prompt * prompt) + epsilon)
    )


def backward_out(
    patch_pre, grad_pooled, noise_level, attended, low_out, w_out, a_out, b_out, w_patch
):
    gelu_back = jax.vjp(jax.nn.gelu, patch_pre)[1]
    grad_pre = gelu_back(jnp.broadcast_to(grad_pooled, patch_pre.shape))[0].astype(jnp.bfloat16)
    grad_denoised = lax.dot_general(
        grad_pre, w_patch, contract_last, preferred_element_type=jnp.float32
    )
    grad_velocity = (-noise_level * grad_denoised).astype(jnp.bfloat16)
    grad_low_out = lax.dot_general(
        grad_velocity, b_out, contract_last, preferred_element_type=jnp.float32
    ).astype(jnp.bfloat16)
    grad_attended = (
        lax.dot_general(grad_velocity, w_out, contract_last, preferred_element_type=jnp.float32)
        + lax.dot_general(grad_low_out, a_out, contract_last, preferred_element_type=jnp.float32)
    ).astype(jnp.bfloat16)
    grad_a_out = lax.dot_general(
        attended, grad_low_out, contract_first, preferred_element_type=jnp.float32
    )
    grad_b_out = lax.dot_general(
        grad_velocity, low_out, contract_first, preferred_element_type=jnp.float32
    )
    return (grad_denoised, grad_attended, grad_a_out, grad_b_out)


MESH = pl.DeviceIdType.MESH
VMEM_LIMIT = 56 * 1024 * 1024
SCALE = HEAD_DIM**-0.5


def normalize(x, gain):
    return x * lax.rsqrt(jnp.mean(x * x, axis=-1, keepdims=True) + epsilon) * gain


def per_head(width):
    return [slice(at, at + HEAD_DIM) for at in range(0, width, HEAD_DIM)]


def attend_kernel(joined_ref, text_ref, gain_ref, att_ref, q_ref, k_ref, v_ref, inv_ref, vt, att_t):
    tokens, width = att_ref.shape
    text = text_ref.shape[1]
    chunk = inv_ref.shape[2]
    gain_q, gain_k = gain_ref[0:1], gain_ref[1:2]
    k_ref[pl.ds(tokens, text), :] = jnp.concatenate(
        [normalize(text_ref[0, :, h].astype(jnp.float32), gain_k) for h in per_head(width)], axis=1
    ).astype(jnp.bfloat16)
    v_ref[pl.ds(tokens, text), :] = text_ref[1]

    @pl.loop(0, tokens // chunk)
    def _(step):
        rows = pl.ds(pl.multiple_of(step * chunk, chunk), chunk)
        part = joined_ref[rows, :]
        q_ref[rows, :] = (
            jnp.concatenate(
                [normalize(part[:, h], gain_q) for h in per_head(width)], axis=1
            ).astype(jnp.bfloat16)
            * SCALE
        ).astype(jnp.bfloat16)
        k_ref[rows, :] = jnp.concatenate(
            [normalize(part[:, width : 2 * width][:, h], gain_k) for h in per_head(width)], axis=1
        ).astype(jnp.bfloat16)
        v_ref[rows, :] = part[:, 2 * width :].astype(jnp.bfloat16)

    vt[...] = v_ref[...].astype(jnp.float32).T.astype(jnp.bfloat16)

    @pl.loop(0, tokens // chunk)
    def _(step):
        rows = pl.ds(pl.multiple_of(step * chunk, chunk), chunk)
        for number, h in enumerate(per_head(width)):
            scores = lax.dot_general(
                k_ref[:, h], q_ref[rows, h], contract_last, preferred_element_type=jnp.float32
            )
            expped = jnp.exp(scores)
            inverse = 1.0 / jnp.sum(expped, axis=0, keepdims=True)
            inv_ref[step, pl.ds(number, 1), :] = inverse
            probs = (expped * inverse).astype(jnp.bfloat16)
            att_t[h, :] = jnp.dot(vt[h, :], probs, preferred_element_type=jnp.float32)
        att_ref[rows, :] = att_t[...].T.astype(jnp.bfloat16)


def attend(joined, text_kv, qk_gain):
    tokens, width = joined.shape[0], joined.shape[1] // 3
    text = text_kv.shape[1]
    chunk = 256 if tokens % 256 == 0 else tokens
    keys = tokens + text
    bf16 = jnp.bfloat16
    whole = pl.BlockSpec(memory_space=pltpu.VMEM)
    return pl.pallas_call(
        attend_kernel,
        out_shape=(
            jax.ShapeDtypeStruct((tokens, width), bf16),
            jax.ShapeDtypeStruct((tokens, width), bf16),
            jax.ShapeDtypeStruct((keys, width), bf16),
            jax.ShapeDtypeStruct((keys, width), bf16),
            jax.ShapeDtypeStruct((tokens // chunk, width // HEAD_DIM, chunk), jnp.float32),
        ),
        in_specs=[whole] * 3,
        out_specs=(whole,) * 5,
        scratch_shapes=[pltpu.VMEM((width, keys), bf16), pltpu.VMEM((width, chunk), jnp.float32)],
        compiler_params=pltpu.CompilerParams(vmem_limit_bytes=VMEM_LIMIT),
        name="attend",
    )(joined, text_kv, qk_gain)


def norm_back(x, gain, grad):
    rounded = grad.astype(jnp.bfloat16).astype(jnp.float32) * gain
    scale = lax.rsqrt(jnp.mean(x * x, axis=-1, keepdims=True) + epsilon)
    along = jnp.mean(rounded * x, axis=-1, keepdims=True)
    return scale * (rounded - x * (scale * scale * along))


def attend_back_kernel(
    joined_ref, q_ref, k_ref, v_ref, inv_ref, g_ref, gain_ref, out_ref, kt, grad_k, grad_v, grad_q
):
    tokens, width = q_ref.shape
    chunk = inv_ref.shape[2]
    gain_q, gain_k = gain_ref[0:1], gain_ref[1:2]
    kt[...] = k_ref[...].astype(jnp.float32).T.astype(jnp.bfloat16)
    grad_k[...] = jnp.zeros_like(grad_k)
    grad_v[...] = jnp.zeros_like(grad_v)

    @pl.loop(0, tokens // chunk)
    def _(step):
        rows = pl.ds(pl.multiple_of(step * chunk, chunk), chunk)
        for number, h in enumerate(per_head(width)):
            query, grad = q_ref[rows, h], g_ref[rows, h]
            scores = lax.dot_general(
                k_ref[:, h], query, contract_last, preferred_element_type=jnp.float32
            )
            probs = jnp.exp(scores) * inv_ref[step, pl.ds(number, 1), :]
            grad_probs = lax.dot_general(
                v_ref[:, h], grad, contract_last, preferred_element_type=jnp.float32
            )
            centre = jnp.sum(probs * grad_probs, axis=0, keepdims=True)
            grad_logits = (probs * (grad_probs - centre)).astype(jnp.bfloat16)
            grad_v[:, h] += jnp.dot(
                probs[:tokens].astype(jnp.bfloat16), grad, preferred_element_type=jnp.float32
            )
            grad_k[:, h] += jnp.dot(
                grad_logits[:tokens], query, preferred_element_type=jnp.float32
            )
            grad_q[h, :] = jnp.dot(kt[h, :], grad_logits, preferred_element_type=jnp.float32)
        back = grad_q[...].T * SCALE
        out_ref[rows, :width] = jnp.concatenate(
            [norm_back(joined_ref[rows, h], gain_q, back[:, h]) for h in per_head(width)], axis=1
        ).astype(jnp.bfloat16)

    @pl.loop(0, tokens // chunk)
    def _(step):
        rows = pl.ds(pl.multiple_of(step * chunk, chunk), chunk)
        part = joined_ref[rows, width : 2 * width]
        back = grad_k[rows, :]
        out_ref[rows, width : 2 * width] = jnp.concatenate(
            [norm_back(part[:, h], gain_k, back[:, h]) for h in per_head(width)], axis=1
        ).astype(jnp.bfloat16)
        out_ref[rows, 2 * width :] = grad_v[rows, :].astype(jnp.bfloat16)


def attend_back(joined, q, k, v, inverse, grad_heads, qk_gain):
    tokens, width = q.shape
    chunk = inverse.shape[2]
    whole = pl.BlockSpec(memory_space=pltpu.VMEM)
    return pl.pallas_call(
        attend_back_kernel,
        out_shape=jax.ShapeDtypeStruct((tokens, 3 * width), jnp.bfloat16),
        in_specs=[whole] * 7,
        out_specs=whole,
        scratch_shapes=[
            pltpu.VMEM((width, k.shape[0]), jnp.bfloat16),
            pltpu.VMEM((tokens, width), jnp.float32),
            pltpu.VMEM((tokens, width), jnp.float32),
            pltpu.VMEM((width, chunk), jnp.float32),
        ],
        compiler_params=pltpu.CompilerParams(vmem_limit_bytes=VMEM_LIMIT),
        name="attend_back",
    )(joined, q, k, v, inverse, grad_heads, qk_gain)


def reduce_kernel(
    sizes, lat_ref, ada_ref, lat_out, ada_out,
    pair_lat, pair_ada, sum_lat, sum_ada, seq_lat, seq_ada, tot_lat, tot_ada,
    part_lat, part_ada, rep_lat, rep_ada, gathered,
    pair_sems, seq_sems, rep_sems, last_sems,
):
    seqs, chips = sizes
    s, r = lax.axis_index("seq"), lax.axis_index("rep")
    z, c = r // 2, lax.rem(r, 2)
    other = 1 - c
    sibling = {"rep": 2 * z + other}
    seq_peers = [lax.rem(s + k, seqs) for k in range(seqs)]
    rep_peers = [lax.rem(z + k, chips) for k in range(chips)]

    barrier = pltpu.get_barrier_semaphore()
    peers = (
        [sibling]
        + [{"seq": p} for p in seq_peers[1:]]
        + [{"rep": 2 * p + c} for p in rep_peers[1:]]
    )
    for peer in peers:
        pl.semaphore_signal(barrier, inc=1, device_id=peer, device_id_type=MESH)
    pl.semaphore_wait(barrier, len(peers))

    def send(source, target, sems, index, peer):
        copy = pltpu.make_async_remote_copy(
            src_ref=source, dst_ref=target, send_sem=sems.at[0, index], recv_sem=sems.at[1, index],
            device_id=peer, device_id_type=MESH,
        )
        copy.start()
        return copy

    order = list(range(1, seqs)) + [0]
    pair_copies = {}
    for k in order:
        to = seq_peers[k]
        pair_copies[k] = (
            send(lat_ref.at[other, to], pair_lat.at[k], pair_sems, 2 * k, sibling),
            send(ada_ref.at[other, to], pair_ada.at[k], pair_sems, 2 * k + 1, sibling),
        )
    f32, bf16 = jnp.float32, jnp.bfloat16
    seq_copies = []
    for k in order:
        to = seq_peers[k]
        for copy in pair_copies[k]:
            copy.wait_recv()
        if k:
            for i in range(chips):
                sum_lat[k - 1, i] = (
                    lat_ref[c, to, i].astype(f32) + pair_lat[k, i].astype(f32)
                ).astype(bf16)
                sum_ada[k - 1, i] = (
                    ada_ref[c, to, i].astype(f32) + pair_ada[k, i].astype(f32)
                ).astype(bf16)
            seq_copies.append(
                send(sum_lat.at[k - 1], seq_lat.at[k - 1], seq_sems, 2 * k - 2, {"seq": to})
            )
            seq_copies.append(
                send(sum_ada.at[k - 1], seq_ada.at[k - 1], seq_sems, 2 * k - 1, {"seq": to})
            )
        else:
            for i in range(chips):
                tot_lat[i] = lat_ref[c, to, i].astype(f32) + pair_lat[k, i].astype(f32)
                tot_ada[i] = ada_ref[c, to, i].astype(f32) + pair_ada[k, i].astype(f32)
    for copy in seq_copies:
        copy.wait_recv()
    rep_copies = []
    for j in list(range(1, chips)) + [0]:
        to = rep_peers[j]
        lat, ada = tot_lat[to], tot_ada[to]
        for k in range(seqs - 1):
            lat += seq_lat[k, to].astype(f32)
            ada += seq_ada[k, to].astype(f32)
        if j:
            part_lat[j - 1] = lat.astype(bf16)
            part_ada[j - 1] = ada.astype(bf16)
            peer = {"rep": 2 * to + c}
            rep_copies.append(
                send(part_ada.at[j - 1], rep_ada.at[j - 1], rep_sems, 2 * j - 1, peer)
            )
            rep_copies.append(
                send(part_lat.at[j - 1], rep_lat.at[j - 1], rep_sems, 2 * j - 2, peer)
            )
        else:
            lat_out[...] = lat
            tot_ada[0] = ada
    for copy in rep_copies:
        copy.wait_recv()
    ada = tot_ada[0]
    for j in range(chips - 1):
        ada += rep_ada[j].astype(f32)
    gathered[s] = ada.astype(bf16)
    last_copies = []
    for k in range(1, seqs):
        last_copies.append(
            send(gathered.at[s], gathered.at[s], last_sems, k - 1, {"seq": seq_peers[k]})
        )
    lat = lat_out[...]
    for j in range(chips - 1):
        lat += rep_lat[j].astype(f32)
    lat_out[...] = lat
    for k in range(1, seqs):
        source = lax.rem(s - k + seqs, seqs)
        pltpu.make_async_remote_copy(
            src_ref=gathered.at[s], dst_ref=gathered.at[source], send_sem=last_sems.at[0, k - 1],
            recv_sem=last_sems.at[1, k - 1], device_id={"seq": source}, device_id_type=MESH,
        ).wait_recv()
    ada_out[...] = gathered[...].astype(f32)
    for copy in [one for pair in pair_copies.values() for one in pair] + seq_copies + rep_copies + last_copies:
        copy.wait_send()


def reduce_all(lat, ada):
    _, seqs, chips, rows, width = lat.shape
    a_rows, lanes = ada.shape[3:]
    bf16, f32 = jnp.bfloat16, jnp.float32
    whole = pl.BlockSpec(memory_space=pltpu.VMEM)

    def both(lead, kind=bf16):
        return [pltpu.VMEM(lead + (rows, width), kind), pltpu.VMEM(lead + (a_rows, lanes), kind)]

    sems = lambda count: pltpu.SemaphoreType.DMA((2, count))
    return pl.pallas_call(
        functools.partial(reduce_kernel, (seqs, chips)),
        out_shape=(
            jax.ShapeDtypeStruct((rows, width), f32),
            jax.ShapeDtypeStruct((seqs, a_rows, lanes), f32),
        ),
        in_specs=[whole] * 2,
        out_specs=(whole,) * 2,
        scratch_shapes=both((seqs, chips)) + both((seqs - 1, chips)) + both((seqs - 1, chips))
        + both((chips,), f32) + both((chips - 1,)) + both((chips - 1,))
        + [pltpu.VMEM((seqs, a_rows, lanes), bf16)]
        + [sems(2 * seqs), sems(2 * seqs - 2), sems(2 * chips - 2), sems(seqs - 1)],
        compiler_params=pltpu.CompilerParams(
            collective_id=0, has_side_effects=True, vmem_limit_bytes=VMEM_LIMIT
        ),
        name="reduce_all",
    )(lat, ada)


def gather_kernel(
    sizes, level_ref, lat_ref, noise_ref, w_ref,
    w_out_ref, normed_ref, dev_ref, mixed_ref,
    lat_all, lat_rows, own_sem, lat_sems, w_sems, norm_sems, dev_sems,
):
    seqs, chips = sizes
    s, r = lax.axis_index("seq"), lax.axis_index("rep")
    z, c = r // 2, lax.rem(r, 2)
    sibling = {"rep": 2 * z + 1 - c}
    ahead = [lax.rem(z + j, chips) for j in range(chips)]
    behind = [lax.rem(z - j + chips, chips) for j in range(chips)]
    seq_ahead = [lax.rem(s + k, seqs) for k in range(seqs)]
    seq_behind = [lax.rem(s - k + seqs, seqs) for k in range(seqs)]
    f32, bf16 = jnp.float32, jnp.bfloat16

    barrier = pltpu.get_barrier_semaphore()
    peers = (
        [sibling]
        + [{"seq": p} for p in seq_ahead[1:]]
        + [{"rep": 2 * p + c} for p in ahead[1:]]
    )
    for peer in peers:
        pl.semaphore_signal(barrier, inc=1, device_id=peer, device_id_type=MESH)
    pl.semaphore_wait(barrier, len(peers))

    def copy(source, target, sems, index, peer):
        return pltpu.make_async_remote_copy(
            src_ref=source, dst_ref=target, send_sem=sems.at[0, index], recv_sem=sems.at[1, index],
            device_id=peer, device_id_type=MESH,
        )

    started = []

    def send(*args):
        one = copy(*args)
        one.start()
        started.append(one)

    for source, target, sems in ((lat_ref, lat_all, lat_sems), (w_ref, w_out_ref, w_sems)):
        for j in range(1, chips):
            send(source, target.at[r], sems, j, {"rep": 2 * ahead[j] + c})
        send(source, target.at[r], sems, chips, sibling)
    own = pltpu.make_async_copy(w_ref, w_out_ref.at[r], own_sem)
    own.start()
    lat_all[r] = lat_ref[...]

    def forward(target, sems):
        for j in range(1, chips):
            block = target.at[2 * behind[j] + c]
            copy(block, block, sems, j, sibling).wait_recv()
            send(block, block, sems, chips + j, sibling)

    def arrive(target, sems):
        for j in range(chips):
            block = target.at[2 * behind[j] + 1 - c]
            copy(block, block, sems, chips + j, sibling).wait_recv()

    forward(lat_all, lat_sems)
    arrive(lat_all, lat_sems)
    length = lat_ref.shape[0]
    rows = noise_ref.shape[0]
    for i in range(2 * chips):
        lat_rows[i * length : (i + 1) * length, :] = lat_all[i].astype(f32)
    level = level_ref[0:1, 0:1]
    chunk = 32 if rows % 32 == 0 else rows

    @pl.loop(0, rows // chunk)
    def _(step):
        at = pl.ds(pl.multiple_of(step * chunk, chunk), chunk)
        mixed = (1.0 - level) * lat_rows[at, :] + level * noise_ref[at, :].astype(f32)
        mixed_ref[at, :] = mixed
        centred = mixed - jnp.mean(mixed, axis=-1, keepdims=True)
        deviation = lax.rsqrt(jnp.mean(centred * centred, axis=-1, keepdims=True) + epsilon)
        normed_ref[s, at, :] = (centred * deviation).astype(bf16)
        dev_ref[s, at, :] = jnp.broadcast_to(deviation, (chunk, dev_ref.shape[2]))

    for k in range(1, seqs):
        send(normed_ref.at[s], normed_ref.at[s], norm_sems, k - 1, {"seq": seq_ahead[k]})
        send(dev_ref.at[s], dev_ref.at[s], dev_sems, k - 1, {"seq": seq_ahead[k]})
    forward(w_out_ref, w_sems)
    own.wait()
    for k in range(1, seqs):
        for target, sems in ((normed_ref, norm_sems), (dev_ref, dev_sems)):
            block = target.at[seq_behind[k]]
            copy(block, block, sems, k - 1, {"seq": seq_ahead[k]}).wait_recv()
    arrive(w_out_ref, w_sems)
    for one in started:
        one.wait_send()


def gather_all(level, latent, noise, weight):
    seqs, reps = lax.axis_size("seq"), lax.axis_size("rep")
    chips = reps // 2
    rows, model = noise.shape
    bf16, f32 = jnp.bfloat16, jnp.float32
    whole = pl.BlockSpec(memory_space=pltpu.VMEM)
    sems = lambda count: pltpu.SemaphoreType.DMA((2, count))
    return pl.pallas_call(
        functools.partial(gather_kernel, (seqs, chips)),
        out_shape=(
            jax.ShapeDtypeStruct((reps,) + weight.shape, bf16),
            jax.ShapeDtypeStruct((seqs, rows, model), bf16),
            jax.ShapeDtypeStruct((seqs, rows, 128), f32),
            jax.ShapeDtypeStruct((rows, model), f32),
        ),
        in_specs=[whole] * 4,
        out_specs=(whole,) * 4,
        scratch_shapes=[
            pltpu.VMEM((reps,) + latent.shape, bf16),
            pltpu.VMEM((rows, model), f32),
            pltpu.SemaphoreType.DMA,
            sems(2 * chips), sems(2 * chips), sems(seqs - 1), sems(seqs - 1),
        ],
        compiler_params=pltpu.CompilerParams(
            collective_id=1, has_side_effects=True, vmem_limit_bytes=VMEM_LIMIT
        ),
        cost_estimate=pl.CostEstimate(flops=10**10, bytes_accessed=2 * 10**8, transcendentals=0),
        name="gather_all",
    )(level, latent, noise, weight)


def shards(
    latent, noise, timestep, text_kv, qk_gain, prompt,
    w_qkv, a_qkv, b_qkv, w_out, a_out, b_out, w_patch,
):
    seqs, reps = lax.axis_size("seq"), lax.axis_size("rep")
    chips = reps // 2
    s = lax.axis_index("seq")
    bf16, f32 = jnp.bfloat16, jnp.float32
    rank = a_qkv.shape[1]
    inner = w_qkv.shape[1] // 3
    width = inner // seqs

    def my_columns(weight):
        return jnp.concatenate(
            [
                lax.dynamic_slice_in_dim(weight, part * inner + s * width, width, 1)
                for part in range(3)
            ],
            axis=1,
        )

    share = w_out.shape[0] // seqs
    w_back = lax.all_gather(
        lax.dynamic_slice_in_dim(w_out, s * share, share, 0), ("rep", "seq"), axis=0, tiled=True
    )
    b_in = my_columns(b_qkv)
    noise_level = timestep[0].astype(f32) / 1000.0
    w_in, normed, deviation, mixed_in = gather_all(
        jnp.full((1, 128), noise_level), latent, noise[0], my_columns(w_qkv)
    )
    w_in = w_in.reshape(-1, 3 * width)
    normed = normed.reshape(-1, normed.shape[2])
    deviation = deviation.reshape(-1, deviation.shape[2])[:, :1]

    low_rank = jnp.dot(normed, a_qkv, preferred_element_type=f32).astype(bf16)
    joined = jnp.dot(normed, w_in, preferred_element_type=f32) + jnp.dot(
        low_rank, b_in, preferred_element_type=f32
    )
    attended_heads, q, k, v, inverse = attend(joined, text_kv, qk_gain)
    attended = lax.all_to_all(attended_heads, "seq", split_axis=0, concat_axis=1, tiled=True)
    low_out, patch_pre, partial_sum = project_out(
        attended, mixed_in, noise_level, w_back, a_out, b_out, w_patch
    )
    pooled = lax.psum(partial_sum, "seq") / normed.shape[0]
    score_value, grad_pooled = jax.value_and_grad(reward)(pooled, prompt)
    grad_denoised, grad_attended, grad_a_out, grad_b_out = backward_out(
        patch_pre, grad_pooled, noise_level, attended, low_out, w_back, a_out, b_out, w_patch
    )
    grad_heads = lax.all_to_all(grad_attended, "seq", split_axis=1, concat_axis=0, tiled=True)
    grad_joined = attend_back(joined, q, k, v, inverse, grad_heads, qk_gain)

    grad_low = lax.dot_general(
        grad_joined, b_in, contract_last, preferred_element_type=f32
    ).astype(bf16)
    grad_normed = lax.dot_general(
        grad_joined, w_in, contract_last, preferred_element_type=f32
    ) + lax.dot_general(grad_low, a_qkv, contract_last, preferred_element_type=f32)
    normed32 = normed.astype(f32)
    grad_mixed = deviation * (
        grad_normed
        - jnp.mean(grad_normed, axis=-1, keepdims=True)
        - normed32 * jnp.mean(grad_normed * normed32, axis=-1, keepdims=True)
    )
    tokens, model = grad_mixed.shape
    rows = tokens // seqs
    mine = (lax.broadcasted_iota(jnp.int32, (seqs, 1, 1), 0) == s).astype(f32)
    grad_mixed = grad_mixed.reshape(seqs, rows, model) + mine * grad_denoised[None]
    lat = ((1.0 - noise_level) * grad_mixed).astype(bf16)
    lat = lat.reshape(seqs, chips, 2, rows // reps, model).transpose(2, 0, 1, 3, 4)

    grad_a_qkv = lax.dot_general(normed, grad_low, contract_first, preferred_element_type=f32)
    grad_b_qkv = lax.dot_general(grad_joined, low_rank, contract_first, preferred_element_type=f32)
    spread = jnp.zeros((3, seqs, width, rank), bf16)
    spread = lax.dynamic_update_slice(
        spread, grad_b_qkv.astype(bf16).reshape(3, 1, width, rank), (0, s, 0, 0)
    )
    by_rep = [
        grad_a_qkv.astype(bf16).reshape(reps, -1, rank),
        spread.reshape(reps, -1, rank),
        grad_a_out.astype(bf16).reshape(reps, -1, rank),
        grad_b_out.astype(bf16).reshape(reps, -1, rank),
    ]
    lengths = [one.shape[1] for one in by_rep]
    ada = jnp.concatenate(by_rep, axis=1)
    half = ada.shape[1] // 2
    ada = jnp.concatenate([ada[:, :half], ada[:, half:]], axis=2)
    ada = ada.reshape(chips, 2, seqs, half // seqs, 2 * rank).transpose(1, 2, 0, 3, 4)
    latent_grad, ada = reduce_all(lat, ada)
    ada = ada.reshape(half, 2 * rank)
    ada = jnp.concatenate([ada[:, :rank], ada[:, rank:]], axis=0)
    pieces, at = [], 0
    for length in lengths:
        pieces.append(ada[at : at + length])
        at += length
    return (
        score_value.reshape(1), latent_grad, pieces[0], pieces[1].T, pieces[2], pieces[3].T,
    )


def solution(mesh):
    in_specs = (
        P(("seq", "rep"), None),
        P("rep", "seq", None),
        P("rep"),
        P(None, None, "seq"),
        P(),
        P(),
        P("rep", None),
        P(),
        P(),
        P("rep", None),
        P(),
        P(),
        P(),
    )
    out_specs = (
        P("rep"),
        P(("seq", "rep"), None),
        P("rep", None),
        P(None, "rep"),
        P("rep", None),
        P(None, "rep"),
    )
    return jax.shard_map(shards, mesh=mesh, in_specs=in_specs, out_specs=out_specs, check_vma=False)
```
